32 devices in a mesh: gx: 4 (over y, x), gy: 2 (over core), gz: 4 (over z).
Axes of the slice: x: 2, y: 2, z: 4, core: 2. Of those that a mesh axis runs over, the one named last changes fastest.
Arguments:
- conductance: float32 [64, 64, 512], P('gx', 'gy', 'gz'), may hold values from 0.1 to 1
- reaction: float32 [64, 64, 512], P('gx', 'gy', 'gz'), may hold values from 0.1 to 1
- source: float32 [64, 64, 512], P('gx', 'gy', 'gz'), may hold values from -8 to 8
Outputs:
- pressure: float32 [64, 64, 512], P('gx', 'gy', 'gz')
- residual: float32 [64, 64, 512], P('gx', 'gy', 'gz')
The draws below stay inside these ranges and needn't reach their ends.
All inputs are finite; a program needn't handle non-finite values.
Results may differ from the reference program's by a relative error of at most 0.0003.
Values sent between devices are 32-bit elements; how exact they have to be, the bound alone decides.
A program may use at most 64 MiB of HBM per device.

```python
import math
import jax
import jax.numpy as jnp

ITERS = 3
NX = 64
NY = 64
NZ = 512


def draw_source(key, part):
    key = jax.random.fold_in(key, 5)
    rough = jax.random.normal(key, (NX, NY, NZ), jnp.float32)
    return jnp.clip(rough, -6.0, 6.0)


def block_levels(key, shape, shards, least, high):
    gain, own = 1.0, jax.random.fold_in(key, 6)
    for position, parts in shards:
        draws = jnp.exp(jax.random.uniform(jax.random.fold_in(own, position), (parts,), jnp.float32, least / len(shards), high / len(shards)))
        gain = gain * jnp.repeat(draws, shape[position] // parts).reshape([-1 if axis == position else 1 for axis in range(len(shape))])
    return gain


def setup_inputs(seed: int = 0) -> dict:
    streams_of = jax.random.split(jax.random.key(seed), 4)
    conductance = jnp.clip(jnp.exp(math.log(1.0) - 2.3025851 * jax.random.uniform(streams_of[0], (NX, NY, NZ), jnp.float32) ** block_levels(streams_of[0], (NX, NY, NZ), ((0, 4), (1, 2), (2, 4)), -0.2, 0.2)), 0.1, 1.0)
    reaction = jnp.clip(jnp.exp(math.log(1.0) - 2.3025851 * jax.random.uniform(streams_of[1], (NX, NY, NZ), jnp.float32) ** block_levels(streams_of[1], (NX, NY, NZ), ((0, 4), (1, 2), (2, 4)), -0.2, 0.2)), 0.1, 1.0)
    source = draw_source(jax.random.fold_in(streams_of[3], 71), 0)
    return dict(conductance=conductance, reaction=reaction, source=source)


chebyshev_low = 0.15
chebyshev_high = 2.0
chebyshev_mid = 0.5 * (chebyshev_high + chebyshev_low)
chebyshev_half = 0.5 * (chebyshev_high - chebyshev_low)
chebyshev_ratio = chebyshev_mid / chebyshev_half
rho_first = 1.0 / chebyshev_ratio
rho_second = 1.0 / (2.0 * chebyshev_ratio - rho_first)
rho_third = 1.0 / (2.0 * chebyshev_ratio - rho_second)
first_scale = 1.0 / chebyshev_mid
keep_second = rho_second * rho_first
push_second = 2.0 * rho_second / chebyshev_half
keep_third = rho_third * rho_second
push_third = 2.0 * rho_third / chebyshev_half


def harmonic(lower_cell, upper_cell):
    summed = lower_cell + upper_cell
    return 2.0 * lower_cell * upper_cell / jnp.where(summed > 0.0, summed, 1.0)


def face_terms(padded, shift_term):
    centre = padded[1:-1, 1:-1, 1:-1]
    uppers = (harmonic(centre, padded[2:, 1:-1, 1:-1]), harmonic(centre, padded[1:-1, 2:, 1:-1]), harmonic(centre, padded[1:-1, 1:-1, 2:]))
    lowers = (harmonic(centre, padded[:-2, 1:-1, 1:-1]), harmonic(centre, padded[1:-1, :-2, 1:-1]), harmonic(centre, padded[1:-1, 1:-1, :-2]))
    diagonal = shift_term + uppers[0] + lowers[0] + uppers[1] + lowers[1] + uppers[2] + lowers[2]
    return uppers, lowers, diagonal


def stencil(padded, operator_terms):
    uppers, lowers, diagonal = operator_terms
    result = diagonal * padded[1:-1, 1:-1, 1:-1]
    result = result - uppers[0] * padded[2:, 1:-1, 1:-1] - lowers[0] * padded[:-2, 1:-1, 1:-1]
    result = result - uppers[1] * padded[1:-1, 2:, 1:-1] - lowers[1] * padded[1:-1, :-2, 1:-1]
    result = result - uppers[2] * padded[1:-1, 1:-1, 2:] - lowers[2] * padded[1:-1, 1:-1, :-2]
    return result


def precondition(vector, operator_terms, inverse):
    update = inverse * vector * first_scale
    approx = update
    residue = vector - stencil(jnp.pad(approx, 1), operator_terms)
    update = keep_second * update + push_second * (inverse * residue)
    approx = approx + update
    residue = vector - stencil(jnp.pad(approx, 1), operator_terms)
    update = keep_third * update + push_third * (inverse * residue)
    return approx + update


def reference(conductance, reaction, source):
    operator_terms = face_terms(jnp.pad(conductance, 1), reaction)
    inverse = 1.0 / operator_terms[2]
    pressure = jnp.zeros_like(source)
    residual = source
    u_vec = precondition(residual, operator_terms, inverse)
    w_vec = stencil(jnp.pad(u_vec, 1), operator_terms)
    z_dir = jnp.zeros_like(source)
    q_dir = jnp.zeros_like(source)
    s_dir = jnp.zeros_like(source)
    p_dir = jnp.zeros_like(source)
    gamma_prev = jnp.float32(1.0)
    alpha_prev = jnp.float32(1.0)
    for iteration in range(ITERS):
        gamma_sum = jnp.sum(residual * u_vec)
        curvature = jnp.sum(w_vec * u_vec)
        m_vec = precondition(w_vec, operator_terms, inverse)
        n_vec = stencil(jnp.pad(m_vec, 1), operator_terms)
        if iteration == 0:
            step_beta = jnp.float32(0.0)
            step_alpha = gamma_sum / curvature
        else:
            step_beta = gamma_sum / gamma_prev
            step_alpha = gamma_sum / (curvature - step_beta * gamma_sum / alpha_prev)
        z_dir = n_vec + step_beta * z_dir
        q_dir = m_vec + step_beta * q_dir
        s_dir = w_vec + step_beta * s_dir
        p_dir = u_vec + step_beta * p_dir
        pressure = pressure + step_alpha * p_dir
        residual = residual - step_alpha * s_dir
        u_vec = u_vec - step_alpha * q_dir
        w_vec = w_vec - step_alpha * z_dir
        gamma_prev = gamma_sum
        alpha_prev = step_alpha
    return pressure, residual
```

```python
import functools

import jax
import jax.numpy as jnp
from jax import lax
from jax.experimental import pallas as pl
from jax.experimental.pallas import tpu as pltpu
from jax.sharding import PartitionSpec as P

ITERS = 3
AXES = ("gx", "gy", "gz")
MESH = pl.DeviceIdType.MESH

chebyshev_low = 0.15
chebyshev_high = 2.0
chebyshev_mid = 0.5 * (chebyshev_high + chebyshev_low)
chebyshev_half = 0.5 * (chebyshev_high - chebyshev_low)
chebyshev_ratio = chebyshev_mid / chebyshev_half
rho_first = 1.0 / chebyshev_ratio
rho_second = 1.0 / (2.0 * chebyshev_ratio - rho_first)
rho_third = 1.0 / (2.0 * chebyshev_ratio - rho_second)
first_scale = 1.0 / chebyshev_mid
keep_second = rho_second * rho_first
push_second = 2.0 * rho_second / chebyshev_half
keep_third = rho_third * rho_second
push_third = 2.0 * rho_third / chebyshev_half

ROUNDS = 1 + 3 * ITERS


def harmonic(a, b):
    return 2.0 * a * b / (a + b)


def conjugate_gradients(moments):
    def product(left, right):
        total = None
        for i, a in enumerate(left):
            for j, b in enumerate(right):
                term = a * b * moments[i + j]
                total = term if total is None else total + term
        return total

    def through_operator(c):
        return [c[0]] + [c[j] - c[j - 1] for j in range(1, len(c))] + [-c[-1]]

    def axpy(x, scale, y):
        out = []
        for j in range(max(len(x), len(y))):
            if j >= len(y):
                out.append(x[j])
            elif j >= len(x):
                out.append(scale * y[j])
            else:
                out.append(x[j] + scale * y[j])
        return out

    residual = [jnp.ones_like(moments[0])]
    pressure, direction = [], []
    gamma_prev = alpha_prev = None
    for iteration in range(ITERS):
        image = through_operator(residual)
        gamma = product(residual, residual)
        curvature = product(image, residual)
        if iteration == 0:
            alpha = gamma / curvature
            direction = list(residual)
        else:
            beta = gamma / gamma_prev
            alpha = gamma / (curvature - beta * gamma / alpha_prev)
            direction = axpy(residual, beta, direction)
        pressure = axpy(pressure, alpha, direction) if pressure else [alpha * d for d in direction]
        residual = axpy(residual, -alpha, through_operator(direction))
        gamma_prev, alpha_prev = gamma, alpha
    return pressure, residual


def kernel(
    sizes,
    cond_hbm, reac_hbm, src_hbm, press_ref, resid_ref,
    cond, reac, src, diag, coef, fields, zs, dvec, hacc,
    halo_x, halo_y, halo_z, stage_y, stage_z, sums_out, sums_in,
    load_sem, send_sem, recv_sem, sum_send, sum_recv,
):
    bx, by, bz = cond.shape
    tiles = by // 8
    me = [lax.axis_index(a) for a in AXES]

    loads = [
        pltpu.make_async_copy(h, v, load_sem.at[i])
        for i, (h, v) in enumerate(((cond_hbm, cond), (reac_hbm, reac), (src_hbm, src)))
    ]
    for load in loads:
        load.start()

    halo_x[...] = jnp.zeros_like(halo_x)
    halo_y[...] = jnp.zeros_like(halo_y)
    halo_z[...] = jnp.zeros_like(halo_z)

    def peer(axis, index):
        return tuple(index if a == axis else me[a] for a in range(3))

    barrier = pltpu.get_barrier_semaphore()
    for axis in range(3):
        for off in range(1, sizes[axis]):
            pl.semaphore_signal(
                barrier, inc=1,
                device_id=peer(axis, lax.rem(me[axis] + off, sizes[axis])),
                device_id_type=MESH,
            )
    pl.semaphore_wait(barrier, sum(s - 1 for s in sizes))

    def face_copy(e, axis, up):
        side = 0 if up else 1
        lane = 2 * axis + side
        if axis == 0:
            plane = bx - 1 if up else 0
            source = fields.at[e, plane]
            target = halo_x.at[e, side]
        elif axis == 1:
            source = stage_y.at[e, side]
            target = halo_y.at[e, side]
        else:
            source = stage_z.at[e]
            target = halo_z.at[e, side]
        return pltpu.make_async_remote_copy(
            src_ref=source, dst_ref=target,
            send_sem=send_sem.at[e, lane], recv_sem=recv_sem.at[e, lane],
            device_id=peer(axis, me[axis] + (1 if up else -1)),
            device_id_type=MESH,
        )

    def exists(axis, up):
        return me[axis] < sizes[axis] - 1 if up else me[axis] > 0

    def send(e, axis):
        for up in (True, False):
            @pl.when(exists(axis, up))
            def _():
                face_copy(e, axis, up).start()

    def receive(e):
        for axis in range(3):
            for up in (True, False):
                @pl.when(exists(axis, not up))
                def _():
                    face_copy(e, axis, up).wait_recv()

    def sent(e):
        for axis in range(3):
            for up in (True, False):
                @pl.when(exists(axis, up))
                def _():
                    face_copy(e, axis, up).wait_send()

    lanes8 = lax.broadcasted_iota(jnp.int32, (8, bz), 1)
    pair8 = lanes8 // 2
    lanes = lax.broadcasted_iota(jnp.int32, (by, bz), 1)
    rows = lax.broadcasted_iota(jnp.int32, (by, bz), 0)
    order = [0, bx - 1] + list(range(1, bx - 1))

    def emit(e, x, plane, packs):
        fields[e, x] = plane
        stage_y[e, 0, pl.ds(x, 1), :] = plane[by - 1:by, :]
        stage_y[e, 1, pl.ds(x, 1), :] = plane[0:1, :]
        for t in range(tiles):
            idx = x * tiles + t
            rolled = pltpu.roll(plane[8 * t:8 * t + 8, :], (2 * idx + 1) % bz, 1)
            packs[t] = jnp.where(pair8 == idx, rolled, packs[t])

    def finish(e, packs):
        total = packs[0]
        for t in range(1, tiles):
            total = jnp.where(pair8 % tiles == t, packs[t], total)
        stage_z[e] = total
        send(e, 2)
        send(e, 1)

    def edge_lanes(e):
        from_upper = pltpu.roll(halo_z[e, 1], bz - 1, 1)
        from_lower = pltpu.roll(halo_z[e, 0], 1, 1)
        return jnp.where(lanes8 % 2 == 0, from_upper, from_lower)

    def neighbours(e, x, edges, plane):
        low_x = fields[e, x - 1] if x > 0 else halo_x[e, 0]
        up_x = fields[e, x + 1] if x < bx - 1 else halo_x[e, 1]
        low_y = jnp.where(rows == 0, halo_y[e, 0, pl.ds(x, 1), :], pltpu.roll(plane, 1, 0))
        up_y = jnp.where(rows == by - 1, halo_y[e, 1, pl.ds(x, 1), :], pltpu.roll(plane, by - 1, 0))
        edge = jnp.concatenate(
            [
                pltpu.roll(edges, (bz - (2 * (x * tiles + t) + 1)) % bz, 1)
                for t in range(tiles)
            ],
            axis=0,
        )
        low_z = jnp.where(lanes == 0, edge, pltpu.roll(plane, 1, 1))
        up_z = jnp.where(lanes == bz - 1, edge, pltpu.roll(plane, bz - 1, 1))
        return low_x, up_x, low_y, up_y, low_z, up_z

    def blank():
        return [jnp.zeros((8, bz), jnp.float32) for _ in range(tiles)]

    loads[0].wait()
    packs = blank()
    for x in order:
        emit(0, x, cond[x], packs)
        if x == bx - 1:
            send(0, 0)
    finish(0, packs)
    loads[1].wait()
    loads[2].wait()
    receive(0)
    edges = edge_lanes(0)
    packs = blank()
    for x in order:
        mine = cond[x]
        faces = [harmonic(mine, other) for other in neighbours(0, x, edges, mine)]
        total = reac[x]
        for face in faces:
            total = total + face
        inverse = 1.0 / total
        diag[x] = total
        for n, face in enumerate(faces):
            coef[n, x] = face * inverse
        first = inverse * src[x]
        zs[0, x] = first
        first = first * first_scale
        dvec[x] = first
        emit(1, x, first, packs)
        if x == bx - 1:
            send(1, 0)
    finish(1, packs)

    def residue(e, k, x, edges):
        plane = fields[e, x]
        total = zs[k, x] - plane
        for n, other in enumerate(neighbours(e, x, edges, plane)):
            total = total + coef[n, x] * other
        return plane, total

    def step(k, last):
        for s, (keep, push) in enumerate(((keep_second, push_second), (keep_third, push_third))):
            e = 3 * k + 1 + s
            receive(e)
            edges = edge_lanes(e)
            packs = blank()
            for x in order:
                plane, rest = residue(e, k, x, edges)
                update = keep * dvec[x] + push * rest
                if s == 0:
                    dvec[x] = update
                emit(e + 1, x, plane + update, packs)
                if x == bx - 1:
                    send(e + 1, 0)
            finish(e + 1, packs)
        e = 3 * k + 3
        receive(e)
        edges = edge_lanes(e)
        packs = blank()
        even = odd = None
        for x in order:
            plane, rest = residue(e, k, x, edges)
            weighted = diag[x] * plane
            a, b = weighted * zs[k, x], weighted * rest
            even = a if even is None else even + a
            odd = b if odd is None else odd + b
            zs[k + 1, x] = rest
            if not last:
                first = rest * first_scale
                dvec[x] = first
                emit(e + 1, x, first, packs)
                if x == bx - 1:
                    send(e + 1, 0)
        if not last:
            finish(e + 1, packs)
        hacc[pl.ds(2 * k, 1), :] = jnp.sum(even, axis=0, keepdims=True)
        hacc[pl.ds(2 * k + 1, 1), :] = jnp.sum(odd, axis=0, keepdims=True)

    hacc[...] = jnp.zeros_like(hacc)

    def body(k, carry):
        step(k, False)
        return carry

    lax.fori_loop(0, ITERS - 1, body, 0)
    step(ITERS - 1, True)

    total = hacc[...]
    base = 0
    for axis in range(3):
        sums_out[axis] = total
        copies = []
        for off in range(1, sizes[axis]):
            slot = base + off - 1
            copies.append(
                pltpu.make_async_remote_copy(
                    src_ref=sums_out.at[axis], dst_ref=sums_in.at[slot],
                    send_sem=sum_send.at[slot], recv_sem=sum_recv.at[slot],
                    device_id=peer(axis, lax.rem(me[axis] + off, sizes[axis])),
                    device_id_type=MESH,
                )
            )
        for copy in copies:
            copy.start()
        for n, copy in enumerate(copies):
            copy.wait_recv()
            total = total + sums_in[base + n]
        for copy in copies:
            copy.wait_send()
        base += sizes[axis] - 1

    row8 = lax.broadcasted_iota(jnp.int32, (8, bz), 0)
    moments = [
        jnp.full((8, bz), jnp.sum(jnp.where(row8 == n, total, 0.0)), jnp.float32)
        for n in range(2 * ITERS)
    ]
    pressure, residual = conjugate_gradients(moments)
    pressure = [jnp.concatenate([c] * tiles, axis=0) for c in pressure]
    residual = [jnp.concatenate([c] * tiles, axis=0) for c in residual]
    for x in range(bx):
        out = pressure[0] * fields[3, x]
        for j in range(1, ITERS):
            out = out + pressure[j] * fields[3 * j + 3, x]
        press_ref[x] = out
        out = residual[0] * zs[0, x]
        for j in range(1, ITERS + 1):
            out = out + residual[j] * zs[j, x]
        resid_ref[x] = diag[x] * out

    for e in range(ROUNDS):
        sent(e)


def solution(mesh):
    sizes = tuple(mesh.shape[a] for a in AXES)
    peers = sum(s - 1 for s in sizes)

    def shards(conductance, reaction, source):
        bx, by, bz = conductance.shape
        block = (bx, by, bz)
        f32 = jnp.float32
        return pl.pallas_call(
            functools.partial(kernel, sizes),
            out_shape=(jax.ShapeDtypeStruct(block, f32),) * 2,
            in_specs=[pl.BlockSpec(memory_space=pl.ANY)] * 3,
            out_specs=(pl.BlockSpec(memory_space=pltpu.VMEM),) * 2,
            scratch_shapes=[
                pltpu.VMEM(block, f32),
                pltpu.VMEM(block, f32),
                pltpu.VMEM(block, f32),
                pltpu.VMEM(block, f32),
                pltpu.VMEM((6,) + block, f32),
                pltpu.VMEM((ROUNDS,) + block, f32),
                pltpu.VMEM((ITERS + 1,) + block, f32),
                pltpu.VMEM(block, f32),
                pltpu.VMEM((8, bz), f32),
                pltpu.VMEM((ROUNDS, 2, by, bz), f32),
                pltpu.VMEM((ROUNDS, 2, bx, bz), f32),
                pltpu.VMEM((ROUNDS, 2, 8, bz), f32),
                pltpu.VMEM((ROUNDS, 2, bx, bz), f32),
                pltpu.VMEM((ROUNDS, 8, bz), f32),
                pltpu.VMEM((3, 8, bz), f32),
                pltpu.VMEM((peers, 8, bz), f32),
                pltpu.SemaphoreType.DMA((3,)),
                pltpu.SemaphoreType.DMA((ROUNDS, 6)),
                pltpu.SemaphoreType.DMA((ROUNDS, 6)),
                pltpu.SemaphoreType.DMA((peers,)),
                pltpu.SemaphoreType.DMA((peers,)),
            ],
            compiler_params=pltpu.CompilerParams(
                collective_id=0, has_side_effects=True,
                vmem_limit_bytes=24 * 1024 * 1024,
            ),
        )(conductance, reaction, source)

    placed = P("gx", "gy", "gz")
    return jax.shard_map(
        shards,
        mesh=mesh,
        in_specs=(placed,) * 3,
        out_specs=(placed,) * 2,
        check_vma=False,
    )
```

```python
import functools

import jax
import jax.numpy as jnp
from jax import lax
from jax.experimental import pallas as pl
from jax.experimental.pallas import tpu as pltpu
from jax.sharding import PartitionSpec as P

ITERS = 3
AXES = ("gx", "gy", "gz")
MESH = pl.DeviceIdType.MESH

chebyshev_low = 0.15
chebyshev_high = 2.0
chebyshev_mid = 0.5 * (chebyshev_high + chebyshev_low)
chebyshev_half = 0.5 * (chebyshev_high - chebyshev_low)
chebyshev_ratio = chebyshev_mid / chebyshev_half
rho_first = 1.0 / chebyshev_ratio
rho_second = 1.0 / (2.0 * chebyshev_ratio - rho_first)
rho_third = 1.0 / (2.0 * chebyshev_ratio - rho_second)
first_scale = 1.0 / chebyshev_mid
keep_second = rho_second * rho_first
push_second = 2.0 * rho_second / chebyshev_half
keep_third = rho_third * rho_second
push_third = 2.0 * rho_third / chebyshev_half

ROUNDS = 1 + 3 * ITERS


def sum_phases(sizes):
    groups = [(1,), (0, 2)] if sizes[0] * sizes[2] <= 32 else [(1,), (0,), (2,)]
    phases = []
    for group in groups:
        spans = [range(sizes[a]) if a in group else range(1) for a in range(3)]
        offsets = [(i, j, k) for i in spans[0] for j in spans[1] for k in spans[2]]
        phases.append(offsets[1:])
    return phases


def harmonic(a, b):
    return 2.0 * a * b / (a + b)


def conjugate_gradients(moments):
    def product(left, right):
        total = None
        for i, a in enumerate(left):
            for j, b in enumerate(right):
                term = a * b * moments[i + j]
                total = term if total is None else total + term
        return total

    def through_operator(c):
        return [c[0]] + [c[j] - c[j - 1] for j in range(1, len(c))] + [-c[-1]]

    def axpy(x, scale, y):
        out = []
        for j in range(max(len(x), len(y))):
            if j >= len(y):
                out.append(x[j])
            elif j >= len(x):
                out.append(scale * y[j])
            else:
                out.append(x[j] + scale * y[j])
        return out

    residual = [jnp.ones_like(moments[0])]
    pressure, direction = [], []
    gamma_prev = alpha_prev = None
    for iteration in range(ITERS):
        image = through_operator(residual)
        gamma = product(residual, residual)
        curvature = product(image, residual)
        if iteration == 0:
            alpha = gamma / curvature
            direction = list(residual)
        else:
            beta = gamma / gamma_prev
            alpha = gamma / (curvature - beta * gamma / alpha_prev)
            direction = axpy(residual, beta, direction)
        pressure = axpy(pressure, alpha, direction) if pressure else [alpha * d for d in direction]
        residual = axpy(residual, -alpha, through_operator(direction))
        gamma_prev, alpha_prev = gamma, alpha
    return pressure, residual


def kernel(
    sizes,
    cond_hbm, reac_hbm, src_hbm, press_ref, resid_ref,
    cond, reac, src, diag, coef, edge_y, edge_z, fields, zs, hacc,
    halo_x, halo_y, halo_z, stage_y, stage_z, sums_out, sums_in,
    load_sem, send_sem, recv_sem, sum_send, sum_recv,
):
    bx, by, bz = cond.shape
    tiles = by // 8
    me = [lax.axis_index(a) for a in AXES]

    loads = [
        pltpu.make_async_copy(h, v, load_sem.at[i])
        for i, (h, v) in enumerate(((cond_hbm, cond), (reac_hbm, reac), (src_hbm, src)))
    ]
    for load in loads:
        load.start()

    halo_x[...] = jnp.zeros_like(halo_x)
    halo_y[...] = jnp.zeros_like(halo_y)
    halo_z[...] = jnp.zeros_like(halo_z)

    def peer(axis, index):
        return tuple(index if a == axis else me[a] for a in range(3))

    phases = sum_phases(sizes)

    def at_offset(offset):
        return tuple(lax.rem(me[a] + offset[a], sizes[a]) if offset[a] else me[a] for a in range(3))

    everyone = sorted({offset for phase in phases for offset in phase} | {
        tuple((o % sizes[a]) if a == axis else 0 for a in range(3))
        for axis in range(3) for o in (1, -1) if sizes[axis] > 1
    })
    barrier = pltpu.get_barrier_semaphore()
    for offset in everyone:
        pl.semaphore_signal(barrier, inc=1, device_id=at_offset(offset), device_id_type=MESH)
    pl.semaphore_wait(barrier, len(everyone))

    def face_copy(e, axis, up):
        side = 0 if up else 1
        lane = 2 * axis + side
        if axis == 0:
            plane = bx - 1 if up else 0
            source = fields.at[e, plane]
            target = halo_x.at[e, side]
        elif axis == 1:
            source = stage_y.at[e, side]
            target = halo_y.at[e, side]
        else:
            source = stage_z.at[e]
            target = halo_z.at[e, side]
        return pltpu.make_async_remote_copy(
            src_ref=source, dst_ref=target,
            send_sem=send_sem.at[e, lane], recv_sem=recv_sem.at[e, lane],
            device_id=peer(axis, me[axis] + (1 if up else -1)),
            device_id_type=MESH,
        )

    def exists(axis, up):
        return me[axis] < sizes[axis] - 1 if up else me[axis] > 0

    def send(e, axis):
        for up in (True, False):
            @pl.when(exists(axis, up))
            def _():
                face_copy(e, axis, up).start()

    def receive(e):
        for axis in range(3):
            for up in (True, False):
                @pl.when(exists(axis, not up))
                def _():
                    face_copy(e, axis, up).wait_recv()

    def sent(e):
        for axis in range(3):
            for up in (True, False):
                @pl.when(exists(axis, up))
                def _():
                    face_copy(e, axis, up).wait_send()

    lanes8 = lax.broadcasted_iota(jnp.int32, (8, bz), 1)
    pair8 = lanes8 // 2
    lanes = lax.broadcasted_iota(jnp.int32, (by, bz), 1)
    rows = lax.broadcasted_iota(jnp.int32, (by, bz), 0)
    order = [0, bx - 1] + list(range(1, bx - 1))

    def pack(x, plane, packs):
        for t in range(tiles):
            idx = x * tiles + t
            rolled = pltpu.roll(plane[8 * t:8 * t + 8, :], (2 * idx + 1) % bz, 1)
            packs[t] = jnp.where(pair8 == idx, rolled, packs[t])

    def merge(packs):
        total = packs[0]
        for t in range(1, tiles):
            total = jnp.where(pair8 % tiles == t, packs[t], total)
        return total

    def emit(e, x, plane, packs):
        fields[e, x] = plane
        stage_y[e, 0, pl.ds(x, 1), :] = plane[by - 1:by, :]
        stage_y[e, 1, pl.ds(x, 1), :] = plane[0:1, :]
        pack(x, plane, packs)

    def finish(e, packs):
        stage_z[e] = merge(packs)
        send(e, 2)
        send(e, 1)

    def edge_lanes(e):
        from_upper = pltpu.roll(halo_z[e, 1], bz - 1, 1)
        from_lower = pltpu.roll(halo_z[e, 0], 1, 1)
        return jnp.where(lanes8 % 2 == 0, from_upper, from_lower)

    def neighbours(e, x, edges, plane):
        low_x = fields[e, x - 1] if x > 0 else halo_x[e, 0]
        up_x = fields[e, x + 1] if x < bx - 1 else halo_x[e, 1]
        low_y = jnp.where(rows == 0, halo_y[e, 0, pl.ds(x, 1), :], pltpu.roll(plane, 1, 0))
        up_y = jnp.where(rows == by - 1, halo_y[e, 1, pl.ds(x, 1), :], pltpu.roll(plane, by - 1, 0))
        edge = jnp.concatenate(
            [
                pltpu.roll(edges, (bz - (2 * (x * tiles + t) + 1)) % bz, 1)
                for t in range(tiles)
            ],
            axis=0,
        )
        low_z = jnp.where(lanes == 0, edge, pltpu.roll(plane, 1, 1))
        up_z = jnp.where(lanes == bz - 1, edge, pltpu.roll(plane, bz - 1, 1))
        return low_x, up_x, low_y, up_y, low_z, up_z

    def blank():
        return [jnp.zeros((8, bz), jnp.float32) for _ in range(tiles)]

    loads[0].wait()
    packs = blank()
    for x in order:
        emit(0, x, cond[x], packs)
        if x == bx - 1:
            send(0, 0)
    finish(0, packs)
    loads[1].wait()
    loads[2].wait()
    receive(0)
    edges = edge_lanes(0)
    packs, edge_packs = blank(), blank()
    for x in order:
        mine = cond[x]
        faces = [harmonic(mine, other) for other in neighbours(0, x, edges, mine)]
        total = reac[x]
        for face in faces:
            total = total + face
        inverse = 1.0 / total
        diag[x] = total
        faces = [face * inverse for face in faces]
        first = inverse * src[x]
        zs[0, x] = first
        emit(1, x, first * first_scale, packs)
        if x == bx - 1:
            send(1, 0)
        coef[0, x] = faces[0]
        coef[1, x] = faces[1]
        edge_y[0, pl.ds(x, 1), :] = faces[2][0:1, :]
        edge_y[1, pl.ds(x, 1), :] = faces[3][by - 1:by, :]
        coef[2, x] = jnp.where(rows == 0, 0.0, faces[2])
        coef[3, x] = jnp.where(rows == by - 1, 0.0, faces[3])
        coef[4, x] = jnp.where(lanes == 0, 0.0, faces[4])
        coef[5, x] = jnp.where(lanes == bz - 1, 0.0, faces[5])
        pack(x, jnp.where(lanes == 0, faces[4], faces[5]), edge_packs)
    finish(1, packs)
    edge_z[...] = merge(edge_packs)

    row8 = lax.broadcasted_iota(jnp.int32, (8, bz), 0)
    ends8 = (lanes8 == 0) | (lanes8 == bz - 1)

    def inner(e, k, x):
        plane = fields[e, x]
        total = zs[k, x] - plane
        if x > 0:
            total = total + coef[0, x] * fields[e, x - 1]
        if x < bx - 1:
            total = total + coef[1, x] * fields[e, x + 1]
        total = total + coef[2, x] * pltpu.roll(plane, 1, 0)
        total = total + coef[3, x] * pltpu.roll(plane, by - 1, 0)
        total = total + coef[4, x] * pltpu.roll(plane, 1, 1)
        total = total + coef[5, x] * pltpu.roll(plane, bz - 1, 1)
        return plane, total

    def outer(e, x, packed):
        pieces = []
        for t in range(tiles):
            shift = (bz - (2 * (x * tiles + t) + 1)) % bz
            piece = jnp.where(ends8, pltpu.roll(packed, shift, 1), 0.0)
            if t == 0:
                row = edge_y[0, pl.ds(x, 1), :] * halo_y[e, 0, pl.ds(x, 1), :]
                piece = piece + jnp.where(row8 == 0, row, 0.0)
            if t == tiles - 1:
                row = edge_y[1, pl.ds(x, 1), :] * halo_y[e, 1, pl.ds(x, 1), :]
                piece = piece + jnp.where(row8 == 7, row, 0.0)
            pieces.append(piece)
        total = jnp.concatenate(pieces, axis=0)
        if x == 0:
            total = total + coef[0, x] * halo_x[e, 0]
        if x == bx - 1:
            total = total + coef[1, x] * halo_x[e, 1]
        return total

    def moment(k, j):
        total = None
        for x in range(bx):
            term = diag[x] * fields[3 * k + 3, x] * zs[j, x]
            total = term if total is None else total + term
        hacc[pl.ds(k + j, 1), :] = jnp.sum(total, axis=0, keepdims=True)

    def step(k, last):
        for s in range(2):
            e = 3 * k + 1 + s
            push = push_third if s else push_second
            for x in range(bx):
                plane, rest = inner(e, k, x)
                before = plane - fields[e - 1, x] if s else plane
                keep = keep_third if s else keep_second
                fields[e + 1, x] = plane + (keep * before + push * rest)
            receive(e)
            packed = edge_z[...] * edge_lanes(e)
            packs = blank()
            for x in order:
                emit(e + 1, x, fields[e + 1, x] + push * outer(e, x, packed), packs)
                if x == bx - 1:
                    send(e + 1, 0)
            finish(e + 1, packs)
        e = 3 * k + 3
        for x in range(bx):
            plane, rest = inner(e, k, x)
            zs[k + 1, x] = rest
        moment(k, k)
        receive(e)
        packed = edge_z[...] * edge_lanes(e)
        packs = blank()
        for x in order:
            rest = zs[k + 1, x] + outer(e, x, packed)
            zs[k + 1, x] = rest
            if not last:
                emit(e + 1, x, rest * first_scale, packs)
                if x == bx - 1:
                    send(e + 1, 0)
        if not last:
            finish(e + 1, packs)
        moment(k, k + 1)

    hacc[...] = jnp.zeros_like(hacc)

    def body(k, carry):
        step(k, False)
        return carry

    lax.fori_loop(0, ITERS - 1, body, 0)
    step(ITERS - 1, True)

    total = hacc[...]
    base = 0
    for n, offsets in enumerate(phases):
        sums_out[n] = total
        copies = []
        for slot, offset in enumerate(offsets, base):
            copies.append(
                pltpu.make_async_remote_copy(
                    src_ref=sums_out.at[n], dst_ref=sums_in.at[slot],
                    send_sem=sum_send.at[slot], recv_sem=sum_recv.at[slot],
                    device_id=at_offset(offset), device_id_type=MESH,
                )
            )
        for copy in copies:
            copy.start()
        for slot, copy in enumerate(copies, base):
            copy.wait_recv()
            total = total + sums_in[slot]
        for copy in copies:
            copy.wait_send()
        base += len(offsets)

    moments = [
        jnp.full((8, bz), jnp.sum(jnp.where(row8 == n, total, 0.0)), jnp.float32)
        for n in range(2 * ITERS)
    ]
    pressure, residual = conjugate_gradients(moments)
    pressure = [jnp.concatenate([c] * tiles, axis=0) for c in pressure]
    residual = [jnp.concatenate([c] * tiles, axis=0) for c in residual]
    for x in range(bx):
        out = pressure[0] * fields[3, x]
        for j in range(1, ITERS):
            out = out + pressure[j] * fields[3 * j + 3, x]
        press_ref[x] = out
        out = residual[0] * zs[0, x]
        for j in range(1, ITERS + 1):
            out = out + residual[j] * zs[j, x]
        resid_ref[x] = diag[x] * out

    for e in range(ROUNDS):
        sent(e)


def solution(mesh):
    sizes = tuple(mesh.shape[a] for a in AXES)
    peers = sum(len(phase) for phase in sum_phases(sizes))

    def shards(conductance, reaction, source):
        bx, by, bz = conductance.shape
        block = (bx, by, bz)
        f32 = jnp.float32
        return pl.pallas_call(
            functools.partial(kernel, sizes),
            out_shape=(jax.ShapeDtypeStruct(block, f32),) * 2,
            in_specs=[pl.BlockSpec(memory_space=pl.ANY)] * 3,
            out_specs=(pl.BlockSpec(memory_space=pltpu.VMEM),) * 2,
            scratch_shapes=[
                pltpu.VMEM(block, f32),
                pltpu.VMEM(block, f32),
                pltpu.VMEM(block, f32),
                pltpu.VMEM(block, f32),
                pltpu.VMEM((6,) + block, f32),
                pltpu.VMEM((2, bx, bz), f32),
                pltpu.VMEM((8, bz), f32),
                pltpu.VMEM((ROUNDS,) + block, f32),
                pltpu.VMEM((ITERS + 1,) + block, f32),
                pltpu.VMEM((8, bz), f32),
                pltpu.VMEM((ROUNDS, 2, by, bz), f32),
                pltpu.VMEM((ROUNDS, 2, bx, bz), f32),
                pltpu.VMEM((ROUNDS, 2, 8, bz), f32),
                pltpu.VMEM((ROUNDS, 2, bx, bz), f32),
                pltpu.VMEM((ROUNDS, 8, bz), f32),
                pltpu.VMEM((3, 8, bz), f32),
                pltpu.VMEM((peers, 8, bz), f32),
                pltpu.SemaphoreType.DMA((3,)),
                pltpu.SemaphoreType.DMA((ROUNDS, 6)),
                pltpu.SemaphoreType.DMA((ROUNDS, 6)),
                pltpu.SemaphoreType.DMA((peers,)),
                pltpu.SemaphoreType.DMA((peers,)),
            ],
            compiler_params=pltpu.CompilerParams(
                collective_id=0, has_side_effects=True,
                vmem_limit_bytes=60 * 1024 * 1024,
            ),
        )(conductance, reaction, source)

    placed = P("gx", "gy", "gz")
    return jax.shard_map(
        shards,
        mesh=mesh,
        in_specs=(placed,) * 3,
        out_specs=(placed,) * 2,
        check_vma=False,
    )
```

```python
import functools

import jax
import jax.numpy as jnp
from jax import lax
from jax.experimental import pallas as pl
from jax.experimental.pallas import tpu as pltpu
from jax.sharding import PartitionSpec as P

ITERS = 3
AXES = ("gx", "gy", "gz")
MESH = pl.DeviceIdType.MESH

chebyshev_low = 0.15
chebyshev_high = 2.0
chebyshev_mid = 0.5 * (chebyshev_high + chebyshev_low)
chebyshev_half = 0.5 * (chebyshev_high - chebyshev_low)
chebyshev_ratio = chebyshev_mid / chebyshev_half
rho_first = 1.0 / chebyshev_ratio
rho_second = 1.0 / (2.0 * chebyshev_ratio - rho_first)
rho_third = 1.0 / (2.0 * chebyshev_ratio - rho_second)
first_scale = 1.0 / chebyshev_mid
keep_second = rho_second * rho_first
push_second = 2.0 * rho_second / chebyshev_half
keep_third = rho_third * rho_second
push_third = 2.0 * rho_third / chebyshev_half

ROUNDS = 1 + 3 * ITERS


def sum_phases(sizes):
    groups = [(1,), (0, 2)] if sizes[0] * sizes[2] <= 32 else [(1,), (0,), (2,)]
    phases = []
    for group in groups:
        spans = [range(sizes[a]) if a in group else range(1) for a in range(3)]
        offsets = [(i, j, k) for i in spans[0] for j in spans[1] for k in spans[2]]
        phases.append(offsets[1:])
    return phases


def harmonic(a, b):
    return 2.0 * a * b / (a + b)


def conjugate_gradients(moments):
    def product(left, right):
        total = None
        for i, a in enumerate(left):
            for j, b in enumerate(right):
                term = a * b * moments[i + j]
                total = term if total is None else total + term
        return total

    def through_operator(c):
        return [c[0]] + [c[j] - c[j - 1] for j in range(1, len(c))] + [-c[-1]]

    def axpy(x, scale, y):
        out = []
        for j in range(max(len(x), len(y))):
            if j >= len(y):
                out.append(x[j])
            elif j >= len(x):
                out.append(scale * y[j])
            else:
                out.append(x[j] + scale * y[j])
        return out

    residual = [jnp.ones_like(moments[0])]
    pressure, direction = [], []
    gamma_prev = alpha_prev = None
    for iteration in range(ITERS):
        image = through_operator(residual)
        gamma = product(residual, residual)
        curvature = product(image, residual)
        if iteration == 0:
            alpha = gamma / curvature
            direction = list(residual)
        else:
            beta = gamma / gamma_prev
            alpha = gamma / (curvature - beta * gamma / alpha_prev)
            direction = axpy(residual, beta, direction)
        pressure = axpy(pressure, alpha, direction) if pressure else [alpha * d for d in direction]
        residual = axpy(residual, -alpha, through_operator(direction))
        gamma_prev, alpha_prev = gamma, alpha
    return pressure, residual


def kernel(
    sizes,
    cond_hbm, reac_hbm, src_hbm, press_ref, resid_ref,
    cond, reac, src, diag, coef, edge_y, edge_z, fields, zs, hacc,
    halo_x, halo_y, halo_z, stage_y, stage_z, sums_out, sums_in,
    load_sem, send_sem, recv_sem, sum_send, sum_recv,
):
    bx, by, bz = cond.shape
    tiles = by // 8
    me = [lax.axis_index(a) for a in AXES]

    loads = [
        pltpu.make_async_copy(h, v, load_sem.at[i])
        for i, (h, v) in enumerate(((cond_hbm, cond), (reac_hbm, reac), (src_hbm, src)))
    ]
    for load in loads:
        load.start()

    halo_x[...] = jnp.zeros_like(halo_x)
    halo_y[...] = jnp.zeros_like(halo_y)
    halo_z[...] = jnp.zeros_like(halo_z)

    def peer(axis, index):
        return tuple(index if a == axis else me[a] for a in range(3))

    phases = sum_phases(sizes)

    def at_offset(offset):
        return tuple(lax.rem(me[a] + offset[a], sizes[a]) if offset[a] else me[a] for a in range(3))

    everyone = sorted({offset for phase in phases for offset in phase} | {
        tuple((o % sizes[a]) if a == axis else 0 for a in range(3))
        for axis in range(3) for o in (1, -1) if sizes[axis] > 1
    })
    barrier = pltpu.get_barrier_semaphore()
    for offset in everyone:
        pl.semaphore_signal(barrier, inc=1, device_id=at_offset(offset), device_id_type=MESH)
    pl.semaphore_wait(barrier, len(everyone))

    def face_copy(e, axis, up):
        side = 0 if up else 1
        lane = 2 * axis + side
        if axis == 0:
            plane = bx - 1 if up else 0
            source = fields.at[e, plane]
            target = halo_x.at[e, side]
        elif axis == 1:
            source = stage_y.at[e, side]
            target = halo_y.at[e, side]
        else:
            source = stage_z.at[e]
            target = halo_z.at[e, side]
        return pltpu.make_async_remote_copy(
            src_ref=source, dst_ref=target,
            send_sem=send_sem.at[e, lane], recv_sem=recv_sem.at[e, lane],
            device_id=peer(axis, me[axis] + (1 if up else -1)),
            device_id_type=MESH,
        )

    def exists(axis, up):
        return me[axis] < sizes[axis] - 1 if up else me[axis] > 0

    def send(e, axis):
        for up in (True, False):
            @pl.when(exists(axis, up))
            def _():
                face_copy(e, axis, up).start()

    def receive(e):
        for axis in range(3):
            for up in (True, False):
                @pl.when(exists(axis, not up))
                def _():
                    face_copy(e, axis, up).wait_recv()

    def sent(e):
        for axis in range(3):
            for up in (True, False):
                @pl.when(exists(axis, up))
                def _():
                    face_copy(e, axis, up).wait_send()

    lanes8 = lax.broadcasted_iota(jnp.int32, (8, bz), 1)
    pair8 = lanes8 // 2
    lanes = lax.broadcasted_iota(jnp.int32, (by, bz), 1)
    rows = lax.broadcasted_iota(jnp.int32, (by, bz), 0)
    order = [0, bx - 1] + list(range(1, bx - 1))

    def pack(x, plane, packs):
        for t in range(tiles):
            idx = x * tiles + t
            rolled = pltpu.roll(plane[8 * t:8 * t + 8, :], (2 * idx + 1) % bz, 1)
            packs[t] = jnp.where(pair8 == idx, rolled, packs[t])

    def merge(packs):
        total = packs[0]
        for t in range(1, tiles):
            total = jnp.where(pair8 % tiles == t, packs[t], total)
        return total

    def emit(e, x, plane, packs):
        fields[e, x] = plane
        stage_y[e, 0, pl.ds(x, 1), :] = plane[by - 1:by, :]
        stage_y[e, 1, pl.ds(x, 1), :] = plane[0:1, :]
        pack(x, plane, packs)

    def finish(e, packs):
        stage_z[e] = merge(packs)
        send(e, 2)
        send(e, 1)

    def edge_lanes(e):
        from_upper = pltpu.roll(halo_z[e, 1], bz - 1, 1)
        from_lower = pltpu.roll(halo_z[e, 0], 1, 1)
        return jnp.where(lanes8 % 2 == 0, from_upper, from_lower)

    def neighbours(e, x, edges, plane):
        low_x = fields[e, x - 1] if x > 0 else halo_x[e, 0]
        up_x = fields[e, x + 1] if x < bx - 1 else halo_x[e, 1]
        low_y = jnp.where(rows == 0, halo_y[e, 0, pl.ds(x, 1), :], pltpu.roll(plane, 1, 0))
        up_y = jnp.where(rows == by - 1, halo_y[e, 1, pl.ds(x, 1), :], pltpu.roll(plane, by - 1, 0))
        edge = jnp.concatenate(
            [
                pltpu.roll(edges, (bz - (2 * (x * tiles + t) + 1)) % bz, 1)
                for t in range(tiles)
            ],
            axis=0,
        )
        low_z = jnp.where(lanes == 0, edge, pltpu.roll(plane, 1, 1))
        up_z = jnp.where(lanes == bz - 1, edge, pltpu.roll(plane, bz - 1, 1))
        return low_x, up_x, low_y, up_y, low_z, up_z

    def blank():
        return [jnp.zeros((8, bz), jnp.float32) for _ in range(tiles)]

    loads[0].wait()
    packs = blank()
    for x in order:
        emit(0, x, cond[x], packs)
        if x == bx - 1:
            send(0, 0)
    finish(0, packs)
    loads[1].wait()
    loads[2].wait()
    receive(0)
    edges = edge_lanes(0)
    packs, edge_packs = blank(), blank()
    for x in order:
        mine = cond[x]
        faces = [harmonic(mine, other) for other in neighbours(0, x, edges, mine)]
        total = reac[x]
        for face in faces:
            total = total + face
        inverse = 1.0 / total
        diag[x] = total
        faces = [face * inverse for face in faces]
        first = inverse * src[x]
        zs[0, x] = first
        emit(1, x, first * first_scale, packs)
        if x == bx - 1:
            send(1, 0)
        coef[0, x] = faces[0]
        coef[1, x] = faces[1]
        edge_y[0, pl.ds(x, 1), :] = faces[2][0:1, :]
        edge_y[1, pl.ds(x, 1), :] = faces[3][by - 1:by, :]
        coef[2, x] = jnp.where(rows == 0, 0.0, faces[2])
        coef[3, x] = jnp.where(rows == by - 1, 0.0, faces[3])
        coef[4, x] = jnp.where(lanes == 0, 0.0, faces[4])
        coef[5, x] = jnp.where(lanes == bz - 1, 0.0, faces[5])
        pack(x, jnp.where(lanes == 0, faces[4], faces[5]), edge_packs)
    finish(1, packs)
    edge_z[...] = merge(edge_packs)

    row8 = lax.broadcasted_iota(jnp.int32, (8, bz), 0)
    ends8 = (lanes8 == 0) | (lanes8 == bz - 1)

    def inner(e, k, x):
        plane = fields[e, x]
        total = zs[k, x] - plane
        if x > 0:
            total = total + coef[0, x] * fields[e, x - 1]
        if x < bx - 1:
            total = total + coef[1, x] * fields[e, x + 1]
        total = total + coef[2, x] * pltpu.roll(plane, 1, 0)
        total = total + coef[3, x] * pltpu.roll(plane, by - 1, 0)
        total = total + coef[4, x] * pltpu.roll(plane, 1, 1)
        total = total + coef[5, x] * pltpu.roll(plane, bz - 1, 1)
        return plane, total

    def outer(e, x, packed):
        pieces = []
        for t in range(tiles):
            shift = (bz - (2 * (x * tiles + t) + 1)) % bz
            piece = jnp.where(ends8, pltpu.roll(packed, shift, 1), 0.0)
            if t == 0:
                row = edge_y[0, pl.ds(x, 1), :] * halo_y[e, 0, pl.ds(x, 1), :]
                piece = piece + jnp.where(row8 == 0, row, 0.0)
            if t == tiles - 1:
                row = edge_y[1, pl.ds(x, 1), :] * halo_y[e, 1, pl.ds(x, 1), :]
                piece = piece + jnp.where(row8 == 7, row, 0.0)
            pieces.append(piece)
        total = jnp.concatenate(pieces, axis=0)
        if x == 0:
            total = total + coef[0, x] * halo_x[e, 0]
        if x == bx - 1:
            total = total + coef[1, x] * halo_x[e, 1]
        return total

    def moment(k, j):
        total = None
        for x in range(bx):
            term = diag[x] * fields[3 * k + 3, x] * zs[j, x]
            total = term if total is None else total + term
        hacc[pl.ds(k + j, 1), :] = jnp.sum(total, axis=0, keepdims=True)

    def step(k, last):
        for s in range(2):
            e = 3 * k + 1 + s
            push = push_third if s else push_second
            for x in range(bx):
                plane, rest = inner(e, k, x)
                before = plane - fields[e - 1, x] if s else plane
                keep = keep_third if s else keep_second
                fields[e + 1, x] = plane + (keep * before + push * rest)
            receive(e)
            packed = edge_z[...] * edge_lanes(e)
            packs = blank()
            for x in order:
                emit(e + 1, x, fields[e + 1, x] + push * outer(e, x, packed), packs)
                if x == bx - 1:
                    send(e + 1, 0)
            finish(e + 1, packs)
        e = 3 * k + 3
        for x in range(bx):
            plane, rest = inner(e, k, x)
            zs[k + 1, x] = rest
        moment(k, k)
        receive(e)
        packed = edge_z[...] * edge_lanes(e)
        packs = blank()
        for x in order:
            rest = zs[k + 1, x] + outer(e, x, packed)
            zs[k + 1, x] = rest
            if not last:
                emit(e + 1, x, rest * first_scale, packs)
                if x == bx - 1:
                    send(e + 1, 0)
        if not last:
            finish(e + 1, packs)
        moment(k, k + 1)

    hacc[...] = jnp.zeros_like(hacc)

    def body(k, carry):
        step(k, False)
        return carry

    lax.fori_loop(0, ITERS - 1, body, 0)
    step(ITERS - 1, True)

    total = hacc[...]
    base = 0
    for n, offsets in enumerate(phases):
        sums_out[n] = total
        copies = []
        for slot, offset in enumerate(offsets, base):
            copies.append(
                pltpu.make_async_remote_copy(
                    src_ref=sums_out.at[n], dst_ref=sums_in.at[slot],
                    send_sem=sum_send.at[slot], recv_sem=sum_recv.at[slot],
                    device_id=at_offset(offset), device_id_type=MESH,
                )
            )
        for copy in copies:
            copy.start()
        for slot, copy in enumerate(copies, base):
            copy.wait_recv()
            total = total + sums_in[slot]
        for copy in copies:
            copy.wait_send()
        base += len(offsets)

    moments = [
        jnp.full((8, bz), jnp.sum(jnp.where(row8 == n, total, 0.0)), jnp.float32)
        for n in range(2 * ITERS)
    ]
    pressure, residual = conjugate_gradients(moments)
    pressure = [jnp.concatenate([c] * tiles, axis=0) for c in pressure]
    residual = [jnp.concatenate([c] * tiles, axis=0) for c in residual]
    for x in range(bx):
        out = pressure[0] * fields[3, x]
        for j in range(1, ITERS):
            out = out + pressure[j] * fields[3 * j + 3, x]
        press_ref[x] = out
        out = residual[0] * zs[0, x]
        for j in range(1, ITERS + 1):
            out = out + residual[j] * zs[j, x]
        resid_ref[x] = diag[x] * out

    for e in range(ROUNDS):
        sent(e)


def solution(mesh):
    sizes = tuple(mesh.shape[a] for a in AXES)
    peers = sum(len(phase) for phase in sum_phases(sizes))

    def shards(conductance, reaction, source):
        bx, by, bz = conductance.shape
        block = (bx, by, bz)
        f32 = jnp.float32
        return pl.pallas_call(
            functools.partial(kernel, sizes),
            out_shape=(jax.ShapeDtypeStruct(block, f32),) * 2,
            in_specs=[pl.BlockSpec(memory_space=pltpu.HBM)] * 3,
            out_specs=(pl.BlockSpec(memory_space=pltpu.VMEM),) * 2,
            scratch_shapes=[
                pltpu.VMEM(block, f32),
                pltpu.VMEM(block, f32),
                pltpu.VMEM(block, f32),
                pltpu.VMEM(block, f32),
                pltpu.VMEM((6,) + block, f32),
                pltpu.VMEM((2, bx, bz), f32),
                pltpu.VMEM((8, bz), f32),
                pltpu.VMEM((ROUNDS,) + block, f32),
                pltpu.VMEM((ITERS + 1,) + block, f32),
                pltpu.VMEM((8, bz), f32),
                pltpu.VMEM((ROUNDS, 2, by, bz), f32),
                pltpu.VMEM((ROUNDS, 2, bx, bz), f32),
                pltpu.VMEM((ROUNDS, 2, 8, bz), f32),
                pltpu.VMEM((ROUNDS, 2, bx, bz), f32),
                pltpu.VMEM((ROUNDS, 8, bz), f32),
                pltpu.VMEM((3, 8, bz), f32),
                pltpu.VMEM((peers, 8, bz), f32),
                pltpu.SemaphoreType.DMA((3,)),
                pltpu.SemaphoreType.DMA((ROUNDS, 6)),
                pltpu.SemaphoreType.DMA((ROUNDS, 6)),
                pltpu.SemaphoreType.DMA((peers,)),
                pltpu.SemaphoreType.DMA((peers,)),
            ],
            compiler_params=pltpu.CompilerParams(
                collective_id=0, has_side_effects=True,
                vmem_limit_bytes=16 * 1024 * 1024,
            ),
        )(*(pltpu.with_memory_space_constraint(a, pltpu.HBM) for a in (conductance, reaction, source)))

    placed = P("gx", "gy", "gz")
    return jax.shard_map(
        shards,
        mesh=mesh,
        in_specs=(placed,) * 3,
        out_specs=(placed,) * 2,
        check_vma=False,
    )
```

```python
import functools

import jax
import jax.numpy as jnp
from jax import lax
from jax.experimental import pallas as pl
from jax.experimental.pallas import tpu as pltpu
from jax.sharding import PartitionSpec as P

ITERS = 3
AXES = ("gx", "gy", "gz")
MESH = pl.DeviceIdType.MESH

chebyshev_low = 0.15
chebyshev_high = 2.0
chebyshev_mid = 0.5 * (chebyshev_high + chebyshev_low)
chebyshev_half = 0.5 * (chebyshev_high - chebyshev_low)
chebyshev_ratio = chebyshev_mid / chebyshev_half
rho_first = 1.0 / chebyshev_ratio
rho_second = 1.0 / (2.0 * chebyshev_ratio - rho_first)
rho_third = 1.0 / (2.0 * chebyshev_ratio - rho_second)
first_scale = 1.0 / chebyshev_mid
keep_second = rho_second * rho_first
push_second = 2.0 * rho_second / chebyshev_half
keep_third = rho_third * rho_second
push_third = 2.0 * rho_third / chebyshev_half

ROUNDS = 1 + 3 * ITERS


def sum_phases(sizes):
    groups = [(1,), (0, 2)] if sizes[0] * sizes[2] <= 32 else [(1,), (0,), (2,)]
    phases = []
    for group in groups:
        spans = [range(sizes[a]) if a in group else range(1) for a in range(3)]
        offsets = [(i, j, k) for i in spans[0] for j in spans[1] for k in spans[2]]
        phases.append(offsets[1:])
    return phases


def harmonic(a, b):
    return 2.0 * a * b / (a + b)


def conjugate_gradients(moments):
    def product(left, right):
        total = None
        for i, a in enumerate(left):
            for j, b in enumerate(right):
                term = a * b * moments[i + j]
                total = term if total is None else total + term
        return total

    def through_operator(c):
        return [c[0]] + [c[j] - c[j - 1] for j in range(1, len(c))] + [-c[-1]]

    def axpy(x, scale, y):
        out = []
        for j in range(max(len(x), len(y))):
            if j >= len(y):
                out.append(x[j])
            elif j >= len(x):
                out.append(scale * y[j])
            else:
                out.append(x[j] + scale * y[j])
        return out

    residual = [jnp.ones_like(moments[0])]
    pressure, direction = [], []
    gamma_prev = alpha_prev = None
    for iteration in range(ITERS):
        image = through_operator(residual)
        gamma = product(residual, residual)
        curvature = product(image, residual)
        if iteration == 0:
            alpha = gamma / curvature
            direction = list(residual)
        else:
            beta = gamma / gamma_prev
            alpha = gamma / (curvature - beta * gamma / alpha_prev)
            direction = axpy(residual, beta, direction)
        pressure = axpy(pressure, alpha, direction) if pressure else [alpha * d for d in direction]
        residual = axpy(residual, -alpha, through_operator(direction))
        gamma_prev, alpha_prev = gamma, alpha
    return pressure, residual


def kernel(
    sizes,
    cond_hbm, reac_hbm, src_hbm, press_ref, resid_ref,
    cond, reac, src, diag, coef, edge_y, edge_z, fields, zs, hacc,
    halo_x, halo_y, halo_z, stage_y, stage_z, sums_out, sums_in,
    load_sem, send_sem, recv_sem, sum_send, sum_recv,
):
    bx, by, bz = cond.shape
    tiles = by // 8
    me = [lax.axis_index(a) for a in AXES]

    loads = [
        pltpu.make_async_copy(h, v, load_sem.at[i])
        for i, (h, v) in enumerate(((cond_hbm, cond), (reac_hbm, reac), (src_hbm, src)))
    ]
    for load in loads:
        load.start()

    halo_x[...] = jnp.zeros_like(halo_x)
    halo_y[...] = jnp.zeros_like(halo_y)
    halo_z[...] = jnp.zeros_like(halo_z)

    def peer(axis, index):
        return tuple(index if a == axis else me[a] for a in range(3))

    phases = sum_phases(sizes)

    def at_offset(offset):
        return tuple(lax.rem(me[a] + offset[a], sizes[a]) if offset[a] else me[a] for a in range(3))

    everyone = sorted({offset for phase in phases for offset in phase} | {
        tuple((o % sizes[a]) if a == axis else 0 for a in range(3))
        for axis in range(3) for o in (1, -1) if sizes[axis] > 1
    })
    barrier = pltpu.get_barrier_semaphore()
    for offset in everyone:
        pl.semaphore_signal(barrier, inc=1, device_id=at_offset(offset), device_id_type=MESH)

    def face_copy(e, axis, up):
        side = 0 if up else 1
        lane = 2 * axis + side
        if axis == 0:
            plane = bx - 1 if up else 0
            source = fields.at[e, plane]
            target = halo_x.at[e, side]
        elif axis == 1:
            source = stage_y.at[e, side]
            target = halo_y.at[e, side]
        else:
            source = stage_z.at[e]
            target = halo_z.at[e, side]
        return pltpu.make_async_remote_copy(
            src_ref=source, dst_ref=target,
            send_sem=send_sem.at[e, lane], recv_sem=recv_sem.at[e, lane],
            device_id=peer(axis, me[axis] + (1 if up else -1)),
            device_id_type=MESH,
        )

    def exists(axis, up):
        return me[axis] < sizes[axis] - 1 if up else me[axis] > 0

    def send(e, axis):
        for up in (True, False):
            @pl.when(exists(axis, up))
            def _():
                face_copy(e, axis, up).start()

    def receive(e):
        for axis in range(3):
            for up in (True, False):
                @pl.when(exists(axis, not up))
                def _():
                    face_copy(e, axis, up).wait_recv()

    def sent(e):
        for axis in range(3):
            for up in (True, False):
                @pl.when(exists(axis, up))
                def _():
                    face_copy(e, axis, up).wait_send()

    lanes8 = lax.broadcasted_iota(jnp.int32, (8, bz), 1)
    pair8 = lanes8 // 2
    lanes = lax.broadcasted_iota(jnp.int32, (by, bz), 1)
    rows = lax.broadcasted_iota(jnp.int32, (by, bz), 0)
    order = [0, bx - 1] + list(range(1, bx - 1))

    def pack(x, plane, packs):
        for t in range(tiles):
            idx = x * tiles + t
            rolled = pltpu.roll(plane[8 * t:8 * t + 8, :], (2 * idx + 1) % bz, 1)
            packs[t] = jnp.where(pair8 == idx, rolled, packs[t])

    def merge(packs):
        total = packs[0]
        for t in range(1, tiles):
            total = jnp.where(pair8 % tiles == t, packs[t], total)
        return total

    def emit(e, x, plane, packs):
        fields[e, x] = plane
        stage_y[e, 0, pl.ds(x, 1), :] = plane[by - 1:by, :]
        stage_y[e, 1, pl.ds(x, 1), :] = plane[0:1, :]
        pack(x, plane, packs)

    def finish(e, packs):
        stage_z[e] = merge(packs)
        send(e, 2)
        send(e, 1)

    def edge_lanes(e):
        from_upper = pltpu.roll(halo_z[e, 1], bz - 1, 1)
        from_lower = pltpu.roll(halo_z[e, 0], 1, 1)
        return jnp.where(lanes8 % 2 == 0, from_upper, from_lower)

    def neighbours(e, x, edges, plane):
        low_x = fields[e, x - 1] if x > 0 else halo_x[e, 0]
        up_x = fields[e, x + 1] if x < bx - 1 else halo_x[e, 1]
        low_y = jnp.where(rows == 0, halo_y[e, 0, pl.ds(x, 1), :], pltpu.roll(plane, 1, 0))
        up_y = jnp.where(rows == by - 1, halo_y[e, 1, pl.ds(x, 1), :], pltpu.roll(plane, by - 1, 0))
        edge = jnp.concatenate(
            [
                pltpu.roll(edges, (bz - (2 * (x * tiles + t) + 1)) % bz, 1)
                for t in range(tiles)
            ],
            axis=0,
        )
        low_z = jnp.where(lanes == 0, edge, pltpu.roll(plane, 1, 1))
        up_z = jnp.where(lanes == bz - 1, edge, pltpu.roll(plane, bz - 1, 1))
        return low_x, up_x, low_y, up_y, low_z, up_z

    def blank():
        return [jnp.zeros((8, bz), jnp.float32) for _ in range(tiles)]

    loads[0].wait()
    packs = blank()
    for x in order:
        emit(0, x, cond[x], packs)
    stage_z[0] = merge(packs)
    pl.semaphore_wait(barrier, len(everyone))
    for axis in (0, 2, 1):
        send(0, axis)
    loads[1].wait()
    loads[2].wait()
    receive(0)
    edges = edge_lanes(0)
    packs, edge_packs = blank(), blank()
    for x in order:
        mine = cond[x]
        faces = [harmonic(mine, other) for other in neighbours(0, x, edges, mine)]
        total = reac[x]
        for face in faces:
            total = total + face
        inverse = 1.0 / total
        diag[x] = total
        faces = [face * inverse for face in faces]
        first = inverse * src[x]
        zs[0, x] = first
        emit(1, x, first * first_scale, packs)
        if x == bx - 1:
            send(1, 0)
        coef[0, x] = faces[0]
        coef[1, x] = faces[1]
        edge_y[0, pl.ds(x, 1), :] = faces[2][0:1, :]
        edge_y[1, pl.ds(x, 1), :] = faces[3][by - 1:by, :]
        coef[2, x] = jnp.where(rows == 0, 0.0, faces[2])
        coef[3, x] = jnp.where(rows == by - 1, 0.0, faces[3])
        coef[4, x] = jnp.where(lanes == 0, 0.0, faces[4])
        coef[5, x] = jnp.where(lanes == bz - 1, 0.0, faces[5])
        pack(x, jnp.where(lanes == 0, faces[4], faces[5]), edge_packs)
    finish(1, packs)
    edge_z[...] = merge(edge_packs)

    row8 = lax.broadcasted_iota(jnp.int32, (8, bz), 0)
    ends8 = (lanes8 == 0) | (lanes8 == bz - 1)

    def inner(e, k, x):
        plane = fields[e, x]
        total = zs[k, x] - plane
        if x > 0:
            total = total + coef[0, x] * fields[e, x - 1]
        if x < bx - 1:
            total = total + coef[1, x] * fields[e, x + 1]
        total = total + coef[2, x] * pltpu.roll(plane, 1, 0)
        total = total + coef[3, x] * pltpu.roll(plane, by - 1, 0)
        total = total + coef[4, x] * pltpu.roll(plane, 1, 1)
        total = total + coef[5, x] * pltpu.roll(plane, bz - 1, 1)
        return plane, total

    def outer(e, x, packed):
        pieces = []
        for t in range(tiles):
            shift = (bz - (2 * (x * tiles + t) + 1)) % bz
            piece = jnp.where(ends8, pltpu.roll(packed, shift, 1), 0.0)
            if t == 0:
                row = edge_y[0, pl.ds(x, 1), :] * halo_y[e, 0, pl.ds(x, 1), :]
                piece = piece + jnp.where(row8 == 0, row, 0.0)
            if t == tiles - 1:
                row = edge_y[1, pl.ds(x, 1), :] * halo_y[e, 1, pl.ds(x, 1), :]
                piece = piece + jnp.where(row8 == 7, row, 0.0)
            pieces.append(piece)
        total = jnp.concatenate(pieces, axis=0)
        if x == 0:
            total = total + coef[0, x] * halo_x[e, 0]
        if x == bx - 1:
            total = total + coef[1, x] * halo_x[e, 1]
        return total

    def moment(k, j):
        total = None
        for x in range(bx):
            term = diag[x] * fields[3 * k + 3, x] * zs[j, x]
            total = term if total is None else total + term
        hacc[pl.ds(k + j, 1), :] = jnp.sum(total, axis=0, keepdims=True)

    def step(k, last):
        for s in range(2):
            e = 3 * k + 1 + s
            push = push_third if s else push_second
            for x in range(bx):
                plane, rest = inner(e, k, x)
                before = plane - fields[e - 1, x] if s else plane
                keep = keep_third if s else keep_second
                fields[e + 1, x] = plane + (keep * before + push * rest)
            receive(e)
            packed = edge_z[...] * edge_lanes(e)
            packs = blank()
            for x in order:
                emit(e + 1, x, fields[e + 1, x] + push * outer(e, x, packed), packs)
                if x == bx - 1:
                    send(e + 1, 0)
            finish(e + 1, packs)
        e = 3 * k + 3
        for x in range(bx):
            plane, rest = inner(e, k, x)
            zs[k + 1, x] = rest
        moment(k, k)
        receive(e)
        packed = edge_z[...] * edge_lanes(e)
        packs = blank()
        odd = None
        for x in order:
            rest = zs[k + 1, x] + outer(e, x, packed)
            zs[k + 1, x] = rest
            if last:
                term = diag[x] * fields[e, x] * rest
                odd = term if odd is None else odd + term
            if not last:
                emit(e + 1, x, rest * first_scale, packs)
                if x == bx - 1:
                    send(e + 1, 0)
        if not last:
            finish(e + 1, packs)
            moment(k, k + 1)
        else:
            hacc[pl.ds(2 * k + 1, 1), :] = jnp.sum(odd, axis=0, keepdims=True)

    hacc[...] = jnp.zeros_like(hacc)

    def body(k, carry):
        step(k, False)
        return carry

    lax.fori_loop(0, ITERS - 1, body, 0)
    step(ITERS - 1, True)

    total = hacc[...]
    base = 0
    for n, offsets in enumerate(phases):
        sums_out[n] = total
        copies = []
        for slot, offset in enumerate(offsets, base):
            copies.append(
                pltpu.make_async_remote_copy(
                    src_ref=sums_out.at[n], dst_ref=sums_in.at[slot],
                    send_sem=sum_send.at[slot], recv_sem=sum_recv.at[slot],
                    device_id=at_offset(offset), device_id_type=MESH,
                )
            )
        for copy in copies:
            copy.start()
        for slot, copy in enumerate(copies, base):
            copy.wait_recv()
            total = total + sums_in[slot]
        for copy in copies:
            copy.wait_send()
        base += len(offsets)

    moments = [
        jnp.full((8, bz), jnp.sum(jnp.where(row8 == n, total, 0.0)), jnp.float32)
        for n in range(2 * ITERS)
    ]
    pressure, residual = conjugate_gradients(moments)
    pressure = [jnp.concatenate([c] * tiles, axis=0) for c in pressure]
    residual = [jnp.concatenate([c] * tiles, axis=0) for c in residual]
    for x in range(bx):
        out = pressure[0] * fields[3, x]
        for j in range(1, ITERS):
            out = out + pressure[j] * fields[3 * j + 3, x]
        press_ref[x] = out
        out = residual[0] * zs[0, x]
        for j in range(1, ITERS + 1):
            out = out + residual[j] * zs[j, x]
        resid_ref[x] = diag[x] * out

    for e in range(ROUNDS):
        sent(e)


def solution(mesh):
    sizes = tuple(mesh.shape[a] for a in AXES)
    peers = sum(len(phase) for phase in sum_phases(sizes))

    def shards(conductance, reaction, source):
        bx, by, bz = conductance.shape
        block = (bx, by, bz)
        f32 = jnp.float32
        return pl.pallas_call(
            functools.partial(kernel, sizes),
            out_shape=(jax.ShapeDtypeStruct(block, f32),) * 2,
            in_specs=[pl.BlockSpec(memory_space=pltpu.HBM)] * 3,
            out_specs=(pl.BlockSpec(memory_space=pltpu.VMEM),) * 2,
            scratch_shapes=[
                pltpu.VMEM(block, f32),
                pltpu.VMEM(block, f32),
                pltpu.VMEM(block, f32),
                pltpu.VMEM(block, f32),
                pltpu.VMEM((6,) + block, f32),
                pltpu.VMEM((2, bx, bz), f32),
                pltpu.VMEM((8, bz), f32),
                pltpu.VMEM((ROUNDS,) + block, f32),
                pltpu.VMEM((ITERS + 1,) + block, f32),
                pltpu.VMEM((8, bz), f32),
                pltpu.VMEM((ROUNDS, 2, by, bz), f32),
                pltpu.VMEM((ROUNDS, 2, bx, bz), f32),
                pltpu.VMEM((ROUNDS, 2, 8, bz), f32),
                pltpu.VMEM((ROUNDS, 2, bx, bz), f32),
                pltpu.VMEM((ROUNDS, 8, bz), f32),
                pltpu.VMEM((3, 8, bz), f32),
                pltpu.VMEM((peers, 8, bz), f32),
                pltpu.SemaphoreType.DMA((3,)),
                pltpu.SemaphoreType.DMA((ROUNDS, 6)),
                pltpu.SemaphoreType.DMA((ROUNDS, 6)),
                pltpu.SemaphoreType.DMA((peers,)),
                pltpu.SemaphoreType.DMA((peers,)),
            ],
            compiler_params=pltpu.CompilerParams(
                collective_id=0, has_side_effects=True,
                vmem_limit_bytes=16 * 1024 * 1024,
            ),
        )(*(pltpu.with_memory_space_constraint(a, pltpu.HBM) for a in (conductance, reaction, source)))

    placed = P("gx", "gy", "gz")
    return jax.shard_map(
        shards,
        mesh=mesh,
        in_specs=(placed,) * 3,
        out_specs=(placed,) * 2,
        check_vma=False,
    )
```
